256 devices in a mesh: trial: 2 (over y_hi), row: 8 (over y_lo, x), col: 16 (over z, core).
Axes of the slice: x: 4, y: 4 (y_hi: 2, y_lo: 2; y = y_hi * 2 + y_lo), z: 8, core: 2. Of those that a mesh axis runs over, the one named last changes fastest.
Arguments:
- layer_input_matrix: bfloat16 [8, 512, 5120], P('trial', 'row', 'col'), may hold values from -6 to 6
- output_gradient_matrix: bfloat16 [8, 512, 25600], P('trial', 'col', 'row'), may hold values from -6 to 6
- fixed_weight_matrix: bfloat16 [5120, 25600], P('col', 'row'), may hold values from -0.078125 to 0.078125
- adapter_left_matrices: bfloat16 [8, 5120, 1024], P('trial', 'col'), may hold values from -0.078125 to 0.078125
- adapter_right_matrices: bfloat16 [8, 1024, 25600], P('trial', 'col', 'row'), may hold values from -0.1875 to 0.1875
- chosen_adapter_entry: int32 [8], P('trial'), may hold values from 0 to 7, as said below
- valid_token_counts: int32 [8], P('trial'), may hold values from 128 to 512, as said below
Outputs:
- grad_input: bfloat16 [8, 512, 5120], P('trial', 'row', 'col')
- grad_a: float32 [8, 5120, 1024], P('trial', 'col', 'row')
- grad_b: float32 [8, 1024, 25600], P('trial', 'col', 'row')
The draws below stay inside these ranges and needn't reach their ends.
Inputs may be any that keep to these rules, and one draw needn't show every extreme that they name: `chosen_adapter_entry`: for each index g of trial, the entries 4 g to 4 g + 3 are a permutation of those same numbers. `valid_token_counts`: every entry is a multiple of 128; some slot has all 512 tokens valid.
All inputs are finite; a program needn't handle non-finite values.
Results may differ from the reference program's by a relative error of at most 0.004.
Values may be sent and summed in bfloat16 or wider, within the bound.
No kernel may reach another device: no remote copies, remote signals or barrier semaphores. Data moves between devices by JAX's collectives and lax.ppermute only.
A program may use at most 128 MiB of HBM per device.

```python
import jax
import jax.numpy as jnp
from jax import lax

D = 5120
FF = 25600
R = 1024
TRIALS_PER_SHARD = 4
SEQ = 512
TRIALS = 8
N_TRIAL = 2


def draw_chosen_adapter_entry(key, part):
    key = jax.random.fold_in(key, 11)
    first, second = jax.random.split(key)
    count = TRIALS_PER_SHARD
    base = jax.random.permutation(first, count).astype(jnp.int32)
    lift = jax.random.randint(second, (N_TRIAL,), 1, count, dtype=jnp.int32)
    groups = jnp.arange(N_TRIAL, dtype=jnp.int32)
    spread = (jnp.cumsum(lift) % count).astype(jnp.int32)
    orders = (base[None, :] + spread[:, None] + groups[:, None] * 0) % count
    orders = jnp.take(base, orders, axis=0)
    offsets = groups[:, None] * count
    return (orders + offsets).reshape(-1).astype(jnp.int32)


def draw_valid_token_counts(key, part):
    key = jax.random.fold_in(key, 23)
    first, second = jax.random.split(key)
    blocks = jax.random.randint(first, (TRIALS,), 1, SEQ // 128 + 1, dtype=jnp.int32)
    full_slot = jax.random.randint(second, (), 0, TRIALS, dtype=jnp.int32)
    slots = jnp.arange(TRIALS, dtype=jnp.int32)
    blocks = jnp.where(slots == full_slot, SEQ // 128, blocks)
    return (blocks * 128).astype(jnp.int32)


def block_scale(stream_key, shape, pieces, least, top_value):
    factor_of, own = 1.0, jax.random.fold_in(stream_key, 6)
    for axis_at, blocks in pieces:
        draws = jnp.exp(jax.random.uniform(jax.random.fold_in(own, axis_at), (blocks,), jnp.float32, least / len(pieces), top_value / len(pieces)))
        factor_of = factor_of * jnp.repeat(draws, shape[axis_at] // blocks).reshape([-1 if axis == axis_at else 1 for axis in range(len(shape))])
    return factor_of


def bell_draw(rng, extent, scale, most, pieces=(), kind=jnp.bfloat16):
    loudness = block_scale(rng, extent, pieces, -0.22, 0.18) if pieces else 1.0
    result = jax.random.normal(rng, extent, jnp.float32) * scale * loudness
    return jnp.minimum(jnp.maximum(result, -most), most).astype(kind)


def setup_inputs(seed: int = 0) -> dict:
    seeds = jax.random.split(jax.random.key(seed), 8)
    layer_input_matrix = bell_draw(seeds[0], (TRIALS, SEQ, D), 1.0, 6.0, ((0, 2), (1, 8), (2, 16)))
    output_gradient_matrix = bell_draw(seeds[1], (TRIALS, SEQ, FF), 1.0, 6.0, ((0, 2), (1, 16), (2, 8)))
    fixed_weight_matrix = bell_draw(seeds[2], (D, FF), D ** -0.5, 0.078125, ((0, 16), (1, 8)))
    adapter_left_matrices = bell_draw(seeds[3], (TRIALS, D, R), D ** -0.5, 0.078125, ((0, 2), (1, 16)))
    adapter_right_matrices = bell_draw(seeds[4], (TRIALS, R, FF), R ** -0.5, 0.1875, ((0, 2), (1, 16), (2, 8)))
    chosen_adapter_entry = draw_chosen_adapter_entry(jax.random.fold_in(seeds[7], 71), 0)
    valid_token_counts = draw_valid_token_counts(jax.random.fold_in(seeds[7], 71), 0)
    return {"layer_input_matrix": layer_input_matrix, "output_gradient_matrix": output_gradient_matrix, "fixed_weight_matrix": fixed_weight_matrix, "adapter_left_matrices": adapter_left_matrices, "adapter_right_matrices": adapter_right_matrices, "chosen_adapter_entry": chosen_adapter_entry, "valid_token_counts": valid_token_counts}


def reference(layer_input_matrix, output_gradient_matrix, fixed_weight_matrix, adapter_left_matrices, adapter_right_matrices, chosen_adapter_entry, valid_token_counts):
    grads_in = []
    grads_a = jnp.zeros(adapter_left_matrices.shape, jnp.float32)
    grads_b = jnp.zeros(adapter_right_matrices.shape, jnp.float32)
    positions = jnp.arange(SEQ, dtype=jnp.int32)
    for experiment_slot_place in range(TRIALS):
        experiment_number = chosen_adapter_entry[experiment_slot_place]
        factor_a = adapter_left_matrices[experiment_number]
        up_factor = adapter_right_matrices[experiment_number]
        upstream = jnp.where((positions < valid_token_counts[experiment_slot_place])[:, None], output_gradient_matrix[experiment_slot_place], jnp.zeros((), output_gradient_matrix.dtype))
        hidden = jnp.dot(layer_input_matrix[experiment_slot_place], factor_a, preferred_element_type=jnp.float32).astype(jnp.bfloat16)
        factor_grad = jnp.dot(upstream, up_factor.T, preferred_element_type=jnp.float32).astype(jnp.bfloat16)
        grad_in = jnp.dot(upstream, fixed_weight_matrix.T, preferred_element_type=jnp.float32) + jnp.dot(factor_grad, factor_a.T, preferred_element_type=jnp.float32)
        grads_in.append(grad_in.astype(jnp.bfloat16))
        scale = lax.rsqrt(valid_token_counts[experiment_slot_place].astype(jnp.float32))
        grads_a = grads_a.at[experiment_number].set(jnp.dot(layer_input_matrix[experiment_slot_place].T, factor_grad, preferred_element_type=jnp.float32) * scale)
        grads_b = grads_b.at[experiment_number].set(jnp.dot(hidden.T, upstream, preferred_element_type=jnp.float32) * scale)
    return (jnp.stack(grads_in), grads_a, grads_b)
```

```python
import jax
import jax.numpy as jnp
from jax import lax
from jax.experimental import pallas as pl
from jax.experimental.pallas import tpu as pltpu
from jax.sharding import PartitionSpec as P

ROWS = 8
PLANES = 8
CORES = 2
F32 = jnp.float32
BF16 = jnp.bfloat16
RING = [(c, (c + 2) % 16) if c % 2 == 0 else (c, (c - 2) % 16) for c in range(16)]
SWAP = [(c, c ^ 1) for c in range(16)]
SAME_CORE = [list(range(0, 16, 2)), list(range(1, 16, 2))]
VMEM_LIMIT = 48 * 1024 * 1024


def dot_last(left, right):
    return lax.dot_general(
        left, right, (((1,), (1,)), ((), ())), preferred_element_type=F32
    )


def dot_first(left, right):
    return lax.dot_general(
        left, right, (((0,), (0,)), ((), ())), preferred_element_type=F32
    )


def step_kernel(*refs):
    units, (w_ref, b_ref, out_ref, rows_ref) = refs[:8], refs[8:]
    height = units[0].shape[0]
    for place, unit in enumerate(units):
        rows_ref[height * place : height * (place + 1), :] = unit[...]
    rows = rows_ref[...]
    main = dot_last(rows, w_ref[...]).astype(BF16)
    side = dot_last(rows, b_ref[...]).astype(BF16)
    feats, ranks = w_ref.shape[0], b_ref.shape[0] // 4
    for place in range(8):
        slot = place % 4
        here = slice(height * place, height * (place + 1))
        out_ref[place, :, :feats] = main[here]
        out_ref[place, :, feats:] = side[here, ranks * slot : ranks * (slot + 1)]


def step_products(units, weight, ups):
    height, depth = units[0].shape
    feats = weight.shape[0]
    ranks = ups.shape[0] // 4
    return pl.pallas_call(
        step_kernel,
        out_shape=jax.ShapeDtypeStruct((8, height, feats + ranks), BF16),
        scratch_shapes=[pltpu.VMEM((8 * height, depth), BF16)],
        compiler_params=pltpu.CompilerParams(vmem_limit_bytes=VMEM_LIMIT),
        cost_estimate=pl.CostEstimate(
            flops=2 * 8 * height * depth * (feats + 4 * ranks),
            bytes_accessed=2 * depth * (8 * height + feats + 4 * ranks),
            transcendentals=0,
        ),
    )(*units, weight, ups)


def grad_b_kernel(slot, place_ref, scale_ref, hidden_ref, *refs):
    units = refs[:16]
    out_ref, hid_ref, rows_ref = refs[-3:]
    height = units[0].shape[0]
    half = hidden_ref.shape[-1] // 2
    plane, core = place_ref[0], place_ref[1]
    lean = 2 * core - 1
    for step in range(8):
        for other in range(2):
            sign = lean if other == 0 else -lean
            origin = (plane + sign * step + 8) % 8
            both = hidden_ref[origin, slot]
            parity = core if other == 0 else 1 - core
            part = jnp.where(parity == 0, both[:, :half], both[:, half:])
            here = slice(height * (2 * step + other), height * (2 * step + other + 1))
            hid_ref[here, :] = part
            rows_ref[here, :] = units[2 * step + other][...]
    out_ref[0] = dot_first(hid_ref[...], rows_ref[...]) * scale_ref[slot]


def grad_b_of(slot, place, scales, hidden, units, done):
    height, depth = units[0].shape
    ranks = hidden.shape[-1] // 2
    block = 640
    smem = pl.BlockSpec(memory_space=pltpu.SMEM)
    extra = [] if done is None else [done]

    def kernel(*refs):
        grad_b_kernel(slot, *refs)

    return pl.pallas_call(
        kernel,
        grid=(depth // block,),
        out_shape=jax.ShapeDtypeStruct((4, ranks, depth), F32),
        in_specs=[smem, smem, pl.BlockSpec(hidden.shape, lambda n: (0, 0, 0, 0))]
        + [pl.BlockSpec((height, block), lambda n: (0, n))] * 16
        + [pl.BlockSpec(memory_space=pl.ANY)] * len(extra),
        out_specs=pl.BlockSpec((1, ranks, block), lambda n: (slot, 0, n)),
        scratch_shapes=[
            pltpu.VMEM((16 * height, ranks), BF16),
            pltpu.VMEM((16 * height, block), BF16),
        ],
        input_output_aliases={19: 0} if extra else {},
        compiler_params=pltpu.CompilerParams(vmem_limit_bytes=VMEM_LIMIT),
        cost_estimate=pl.CostEstimate(
            flops=2 * 16 * height * depth * ranks,
            bytes_accessed=2 * 16 * height * depth + 4 * ranks * depth,
            transcendentals=0,
        ),
    )(place, scales, hidden, *units, *extra)


def by_destination(parts, plane):
    doubled = jnp.concatenate(parts + parts, axis=0)
    return lax.dynamic_slice_in_dim(doubled, (8 - plane) % 8, 8, axis=0)


def body(x, dy, weight, lefts, rights, chosen, counts):
    slots, tokens, feats = x.shape
    height, depth = dy.shape[1:]
    ranks = rights.shape[1]
    col = lax.axis_index("col")
    row = lax.axis_index("row")
    plane, core = col // 2, col % 2
    entry = chosen - lax.axis_index("trial") * slots
    order = jnp.arange(slots, dtype=jnp.int32)
    slot_of = jnp.sum(jnp.where(entry[None, :] == order[:, None], order[None, :], 0), axis=1)
    lengths = counts[slot_of]
    scales = lax.rsqrt(lengths.astype(F32))
    x = jnp.take(x, slot_of, axis=0)

    units = [lax.dynamic_index_in_dim(dy, slot_of[j], 0, keepdims=False) for j in range(slots)]
    own, sibling = [units], []
    for step in range(1, PLANES):
        own.append([lax.ppermute(unit, "col", RING) for unit in own[-1]])
    for step in range(PLANES):
        sibling.append([lax.ppermute(unit, "col", SWAP) for unit in own[step]])

    ups = rights.reshape(slots * ranks, depth)
    even, odd = [], []
    for step in range(PLANES):
        product = step_products(own[step] + sibling[step], weight, ups)
        mine, others = product[:slots], product[slots:]
        even.append(jnp.where(core == 0, mine, others)[None])
        odd.append(jnp.where(core == 0, others, mine)[None])
    first = [even[0], odd[1], odd[2], odd[3], odd[4], even[3], even[2], even[1]]
    second = [odd[0], even[7], even[6], even[5], even[4], odd[5], odd[6], odd[7]]
    sums = []
    for parts in (first, second):
        terms = lax.all_to_all(by_destination(parts, plane), "row", 0, 0)
        sums.append(jnp.sum(terms.astype(F32), axis=0))
    away = (row - plane) % 8
    first_even = (away == 0) | (away >= 5)
    sum_even = jnp.where(first_even, sums[0], sums[1])
    sum_odd = jnp.where(first_even, sums[1], sums[0])
    total = jnp.stack([sum_even, sum_odd], axis=1)
    position = tokens * row + jnp.arange(tokens, dtype=jnp.int32).reshape(1, 2, height)
    valid = position < lengths[:, None, None]
    total = jnp.where(valid[..., None], total, 0.0)
    main = total[..., :feats]
    factor = jnp.concatenate(
        [total[:, 0, :, feats:], total[:, 1, :, feats:]], axis=-1
    ).astype(BF16)

    def over_planes(piece):
        spread = jnp.broadcast_to(piece[None], (PLANES,) + piece.shape)
        return lax.all_to_all(spread, "col", 0, 0, axis_index_groups=SAME_CORE)

    def both_cores(piece):
        other = lax.ppermute(piece, "col", SWAP)
        return jnp.where(core == 0, piece, other), jnp.where(core == 0, other, piece)

    factor_planes = over_planes(factor)
    factor_tokens = lax.all_to_all(factor_planes, "row", 0, 0)

    def split(piece):
        return piece.reshape(piece.shape[:-1] + (2, ranks))

    low, high = both_cores(factor_planes)
    wide = jnp.stack([split(low), split(high)], axis=0)
    wide = wide.transpose(2, 4, 3, 1, 0, 5).reshape(slots, tokens, PLANES * CORES * ranks)
    side = lax.dot_general(
        wide, lefts, (((2,), (2,)), ((0,), (0,))), preferred_element_type=F32
    )
    grad_in = (main.reshape(slots, tokens, feats) + side).astype(BF16)
    grad_in = jnp.take(grad_in, entry, axis=0)

    low, high = both_cores(factor_tokens)
    tall = jnp.stack([split(low), split(high)], axis=0)
    tall = tall.transpose(2, 1, 4, 3, 0, 5).reshape(slots, ROWS * tokens, CORES * ranks)
    x_spread = jnp.broadcast_to(x[None], (ROWS,) + x.shape)
    x_all = lax.all_to_all(x_spread, "row", 0, 0)
    x_all = x_all.transpose(1, 0, 2, 3).reshape(slots, ROWS * tokens, feats)
    grad_a = lax.dot_general(
        x_all, tall, (((1,), (1,)), ((0,), (0,))), preferred_element_type=F32
    )
    grad_a = grad_a * scales[:, None, None]

    partial = lax.dot_general(
        x, lefts, (((2,), (1,)), ((0,), (0,))), preferred_element_type=F32
    )
    partial = partial.reshape(slots, 2, height, PLANES, CORES, ranks)
    partial = partial.transpose(4, 3, 0, 2, 1, 5).reshape(CORES, PLANES, slots, height, 2 * ranks)
    keep = lax.dynamic_index_in_dim(partial, core, 0, keepdims=False)
    give = lax.dynamic_index_in_dim(partial, 1 - core, 0, keepdims=False)
    keep = keep + lax.ppermute(give, "col", SWAP)
    terms = lax.all_to_all(keep.astype(BF16), "col", 0, 0, axis_index_groups=SAME_CORE)
    hidden = jnp.sum(terms.astype(F32), axis=0)
    lanes = jnp.repeat(jnp.swapaxes(valid, 1, 2), ranks, axis=2)
    hidden = jnp.where(lanes, hidden, 0.0).astype(BF16)
    hidden = lax.all_to_all(
        jnp.broadcast_to(hidden[None], (ROWS,) + hidden.shape), "row", 0, 0
    )

    place = jnp.stack([plane, core]).astype(jnp.int32)
    grad_b = None
    for j in range(slots):
        chunks = []
        for step in range(PLANES):
            chunks += [own[step][j], sibling[step][j]]
        grad_b = grad_b_of(j, place, scales, hidden, chunks, grad_b)
    return grad_in, grad_a, grad_b


def solution(mesh):
    return jax.shard_map(
        body,
        mesh=mesh,
        in_specs=(
            P("trial", "row", "col"),
            P("trial", "col", "row"),
            P("col", "row"),
            P("trial", "col", None),
            P("trial", "col", "row"),
            P("trial"),
            P("trial"),
        ),
        out_specs=(P("trial", "row", "col"), P("trial", "col", "row"), P("trial", "col", "row")),
        check_vma=False,
    )
```

```python
import jax
import jax.numpy as jnp
from jax import lax
from jax.experimental import pallas as pl
from jax.experimental.pallas import tpu as pltpu
from jax.sharding import PartitionSpec as P

ROWS = 8
PLANES = 8
SLOTS = 4
CHAINS = 2
F32 = jnp.float32
BF16 = jnp.bfloat16
RING = [(c, (c + 2) % 16) if c % 2 == 0 else (c, (c - 2) % 16) for c in range(16)]
SWAP = [(c, c ^ 1) for c in range(16)]
SAME_CORE = [list(range(0, 16, 2)), list(range(1, 16, 2))]
SMEM = pl.BlockSpec(memory_space=pltpu.SMEM)
VMEM = pl.BlockSpec(memory_space=pltpu.VMEM)
ANY = pl.BlockSpec(memory_space=pl.ANY)
MIB = 1024 * 1024
GUESS = pl.CostEstimate(flops=3 * 10**9, bytes_accessed=8 * MIB, transcendentals=0)


def dot_last(left, right):
    return lax.dot_general(
        left, right, (((1,), (1,)), ((), ())), preferred_element_type=F32
    )


def dot_first(left, right):
    return lax.dot_general(
        left, right, (((0,), (0,)), ((), ())), preferred_element_type=F32
    )


def origin_of(place, step):
    return lax.rem(place[0] + (2 * place[1] - 1) * step + PLANES, PLANES)


def keep_kernel(*refs):
    sems, refs = refs[-1], refs[:-1]
    count = len(refs) // 2
    copies = [
        pltpu.make_async_copy(refs[n], refs[count + n], sems.at[n]) for n in range(count)
    ]
    for copy in copies:
        copy.start()
    for copy in copies:
        copy.wait()


def kept_in_vmem(arrays):
    return pl.pallas_call(
        keep_kernel,
        out_shape=tuple(pltpu.VMEM(array.shape, array.dtype) for array in arrays),
        in_specs=[ANY] * len(arrays),
        out_specs=(VMEM,) * len(arrays),
        scratch_shapes=[pltpu.SemaphoreType.DMA((len(arrays),))],
        compiler_params=pltpu.CompilerParams(vmem_limit_bytes=24 * MIB),
        cost_estimate=GUESS,
    )(*arrays)


def step_kernel(steps, place, *refs):
    count = CHAINS * len(steps)
    units, weights = refs[:count], refs[count : count + 4]
    main_out, side_out, acc_c, acc_d, main, side, sems = refs[-7:]
    height = units[0].shape[1]
    rows = jnp.concatenate(
        [unit[n] for unit in units for n in range(SLOTS // CHAINS)], axis=0
    )
    acc_a = dot_last(rows, weights[0][...])
    acc_b = dot_last(rows, weights[1][...])
    for at in range(len(steps)):
        for slot in range(SLOTS):
            top = height * (SLOTS * at + slot)
            here = slice(top, top + height)
            both = jnp.concatenate([acc_a[here], acc_b[here]], axis=1)
            main[at, slot] = both.astype(BF16)
    copies = [
        pltpu.make_async_copy(
            main.at[at], main_out.at[origin_of(place, step)], sems.at[2 * at]
        )
        for at, step in enumerate(steps)
    ]
    for copy in copies:
        copy.start()
    acc_c[...] = dot_last(rows, weights[2][...])
    acc_d[...] = dot_last(rows, weights[3][...])
    half = acc_c.shape[1] // SLOTS
    for at, step in enumerate(steps):
        for slot in range(SLOTS):
            top = height * (SLOTS * at + slot)
            here = slice(top, top + height)
            entry = place[2 + slot]
            lanes = pl.ds(pl.multiple_of(entry // 2 * 2 * half, 2 * half), 2 * half)
            parts = []
            for acc in (acc_c, acc_d):
                pair = acc[here, lanes]
                parts.append(jnp.where(entry % 2 == 0, pair[:, :half], pair[:, half:]))
            side[at, slot] = jnp.concatenate(parts, axis=1).astype(BF16)
        copy = pltpu.make_async_copy(
            side.at[at], side_out.at[origin_of(place, step)], sems.at[1 + 2 * at]
        )
        copy.start()
        copies.append(copy)
    for copy in copies:
        copy.wait()


def step_products(steps, place, units, weights, done):
    height = units[0].shape[1]
    feats, ranks = weights[0].shape[0], weights[2].shape[0]
    count = len(units)
    rows = SLOTS * len(steps) * height
    main_shape = (SLOTS, height, 2 * feats)
    side_shape = (SLOTS, height, 2 * ranks // SLOTS)

    def kernel(*refs):
        step_kernel(steps, *refs)

    return pl.pallas_call(
        kernel,
        out_shape=(
            jax.ShapeDtypeStruct((ROWS,) + main_shape, BF16),
            jax.ShapeDtypeStruct((ROWS,) + side_shape, BF16),
        ),
        in_specs=[SMEM] + [VMEM] * (count + 4) + [ANY] * len(done),
        out_specs=(ANY, ANY),
        scratch_shapes=[
            pltpu.VMEM((rows, ranks), F32),
            pltpu.VMEM((rows, ranks), F32),
            pltpu.VMEM((len(steps),) + main_shape, BF16),
            pltpu.VMEM((len(steps),) + side_shape, BF16),
            pltpu.SemaphoreType.DMA((2 * len(steps),)),
        ],
        input_output_aliases={count + 5: 0, count + 6: 1} if done else {},
        compiler_params=pltpu.CompilerParams(vmem_limit_bytes=24 * MIB),
        cost_estimate=GUESS,
    )(place, *units, *weights, *done)


def small_call(kernel, out_shape, args, scratch=(), limit=24):
    scalars = sum(arg.ndim == 1 for arg in args)
    return pl.pallas_call(
        kernel,
        out_shape=out_shape,
        in_specs=[SMEM] * scalars + [VMEM] * (len(args) - scalars),
        out_specs=jax.tree.map(lambda _: VMEM if not scratch else ANY, out_shape),
        scratch_shapes=list(scratch),
        compiler_params=pltpu.CompilerParams(vmem_limit_bytes=limit * MIB),
        cost_estimate=GUESS,
    )(*args)


def pick(place, low, high):
    first = place[1] == 0
    return jnp.where(first, low, high), jnp.where(first, high, low)


def own_rows(place, height):
    start = pl.multiple_of(place[1] * height, height)
    return pl.ds(start, height)


def other_rows(place, height):
    start = pl.multiple_of((1 - place[1]) * height, height)
    return pl.ds(start, height)


def masked_sum(place, terms, slot):
    total = terms[0, slot].astype(F32)
    for source in range(1, ROWS):
        total = total + terms[source, slot].astype(F32)
    height = total.shape[0]
    start = 2 * height * place[6] + height * place[1]
    position = start + lax.broadcasted_iota(jnp.int32, total.shape, 0)
    return jnp.where(position < place[7 + slot], total, 0.0)


def send_to_all(stage, out, sems):
    copies = [pltpu.make_async_copy(stage, out.at[n], sems.at[n]) for n in range(8)]
    for copy in copies:
        copy.start()
    for copy in copies:
        copy.wait()


def hidden_kernel(place, x, lefts, keep, give):
    height, width = keep.shape[2:]
    for slot in range(SLOTS):
        both = jnp.dot(x[slot], lefts[place[2 + slot]], preferred_element_type=F32)
        mine, others = pick(place, both[:height], both[height:])
        for plane in range(PLANES):
            lanes = slice(width * plane, width * (plane + 1))
            keep[plane, slot] = mine[:, lanes]
            give[plane, slot] = others[:, lanes]


def share_kernel(place, terms, x, out, stage, sems):
    for slot in range(SLOTS):
        hidden = masked_sum(place, terms, slot).astype(BF16)
        half = hidden.shape[1] // 2
        stacked = jnp.concatenate([hidden[:, :half], hidden[:, half:]], axis=0)
        stage[slot] = jnp.concatenate([x[slot], stacked], axis=1)
    send_to_all(stage, out, sems)


def factor_kernel(place, terms, out):
    for slot in range(SLOTS):
        total = masked_sum(place, terms, slot)
        half = total.shape[1] // 2
        turned = jnp.concatenate([total[:, half:], total[:, :half]], axis=1)
        out[slot] = jnp.where(place[1] == 0, total, turned).astype(BF16)


def stack_kernel(place, *refs):
    pieces, (out, sems) = refs[:PLANES], refs[PLANES:]
    copies = []
    for hop, piece in enumerate(pieces):
        origin = lax.rem(place[0] - hop + PLANES, PLANES)
        copies.append(pltpu.make_async_copy(piece, out.at[origin], sems.at[hop]))
    for copy in copies:
        copy.start()
    for copy in copies:
        copy.wait()


def main_kernel(place, terms, keep, give):
    feats = keep.shape[-1]
    for slot in range(SLOTS):
        total = masked_sum(place, terms, slot)
        keep[slot] = total[:, :feats]
        give[slot] = total[:, feats:]


def grad_in_kernel(place, mine, others, keep, got, lefts, out):
    height = keep.shape[1]
    for slot in range(SLOTS):
        rows = jnp.concatenate(
            [
                jnp.concatenate([part[plane, slot] for plane in range(PLANES)], axis=1)
                for part in (mine, others)
            ],
            axis=0,
        )
        side = dot_last(rows, lefts[place[2 + slot]])
        out[slot, own_rows(place, height)] = (keep[slot] + side[:height]).astype(BF16)
        out[slot, other_rows(place, height)] = (got[slot] + side[height:]).astype(BF16)


def grad_a_kernel(place, scales, mine, others, shared, out):
    height = mine.shape[2]
    feats = out.shape[1]
    for slot in range(SLOTS):
        acts, factors = [], []
        for part, here in (
            (mine, own_rows(place, height)),
            (others, other_rows(place, height)),
        ):
            for row in range(ROWS):
                acts.append(shared[row, slot, here, :feats])
                factors.append(part[row, slot])
        acts = jnp.concatenate(acts, axis=0)
        factors = jnp.concatenate(factors, axis=0)
        out[place[2 + slot]] = dot_first(acts, factors) * scales[slot]


def grad_b_kernel(place, scales, shared, *refs):
    units, (keep, give, rows, sems) = refs[:-4], refs[-4:]
    ranks = keep.shape[1]
    height = units[0].shape[1]
    feats = shared.shape[-1] - ranks
    loads = []
    for slot in range(SLOTS):
        for step in range(PLANES):
            here = pl.ds(height * step, height)
            pair = SLOTS // CHAINS
            unit = units[CHAINS * step + slot // pair].at[slot % pair]
            sem = sems.at[PLANES * slot + step]
            loads.append(pltpu.make_async_copy(unit, rows.at[slot, here], sem))
    for load in loads:
        load.start()
    for slot in range(SLOTS):
        hidden = []
        for step in range(PLANES):
            origin = origin_of(place, step)
            pair = [
                shared[origin, slot, here, feats:]
                for here in (own_rows(place, height), other_rows(place, height))
            ]
            hidden.append(jnp.concatenate(pair, axis=1))
            loads[PLANES * slot + step].wait()
        both = dot_first(jnp.concatenate(hidden, axis=0), rows[slot]) * scales[slot]
        entry = place[2 + slot]
        keep[entry] = both[:ranks]
        give[entry] = both[ranks:]


def grad_b_parts(place, scales, shared, units):
    height, depth = units[0].shape[1:]
    ranks = shared.shape[2]
    part = jax.ShapeDtypeStruct((SLOTS, ranks, depth), F32)
    return pl.pallas_call(
        grad_b_kernel,
        out_shape=(part, part),
        in_specs=[SMEM, SMEM, VMEM] + [ANY] * len(units),
        out_specs=(VMEM, VMEM),
        scratch_shapes=[
            pltpu.VMEM((SLOTS, PLANES * height, depth), BF16),
            pltpu.SemaphoreType.DMA((SLOTS * PLANES,)),
        ],
        compiler_params=pltpu.CompilerParams(vmem_limit_bytes=60 * MIB),
        cost_estimate=GUESS,
    )(place, scales, shared, *units)


def body(x, dy, weight, lefts, rights, chosen, counts):
    slots, tokens, feats = x.shape
    height, depth = dy.shape[1:]
    ranks = rights.shape[1]
    col = lax.axis_index("col")
    row = lax.axis_index("row")
    plane, core = col // 2, col % 2

    def swap(piece):
        return lax.ppermute(piece, "col", SWAP)

    def over_planes(pieces):
        return lax.all_to_all(pieces, "col", 0, 0, axis_index_groups=SAME_CORE)

    def over_rows(pieces):
        return lax.all_to_all(pieces, "row", 0, 0)

    def after(value, *earlier):
        return lax.optimization_barrier((value,) + earlier)[0]

    def passed_on(units):
        return [lax.ppermute(unit, "col", RING) for unit in units]

    shape = jax.ShapeDtypeStruct
    sems = pltpu.SemaphoreType.DMA((8,))
    entry = chosen - lax.axis_index("trial") * slots
    scales = lax.rsqrt(counts.astype(F32))
    place = jnp.concatenate([jnp.stack([plane, core]), entry, row[None], counts])
    place = place.astype(jnp.int32)

    pair = slots // CHAINS
    own = [[dy[pair * n : pair * (n + 1)] for n in range(CHAINS)]]
    own.append(passed_on(own[0]))
    ups = after(rights.reshape(slots * ranks, depth), *own[1])
    weight = after(weight, *own[1])
    weights = [weight, swap(weight), ups, swap(ups)]
    own.append(passed_on(own[1]))

    piece = (PLANES, slots, height, 2 * ranks)
    keep, give = small_call(
        hidden_kernel,
        (shape(piece, F32), shape(piece, F32)),
        (place, after(x, own[1][0]), lefts),
    )
    terms = over_planes((keep + swap(give)).astype(BF16))
    own.append(passed_on(own[2]))
    weights = kept_in_vmem(weights)
    products = step_products((0, 1), place, own[0] + own[1], weights, ())
    own[3][0] = after(own[3][0], *products)
    own.append(passed_on(own[3]))
    wide = (slots, tokens, feats + ranks)
    shared = small_call(
        share_kernel,
        shape((ROWS,) + wide, BF16),
        (place, terms, x),
        scratch=(pltpu.VMEM(wide, BF16), sems),
    )
    shared = over_rows(shared)
    own.append(passed_on(own[4]))
    products = step_products((2, 3), place, own[2] + own[3], weights, products)
    own[5][0] = after(own[5][0], *products)
    own.append(passed_on(own[5]))
    products = step_products((4, 5), place, own[4] + own[5], weights, products)
    own[6][1] = after(own[6][1], *products)
    own.append(passed_on(own[6]))
    products = step_products((6, 7), place, own[6] + own[7], weights, products)
    main_parts, side_parts = products

    side_terms = over_rows(after(side_parts, shared))
    keep_b, give_b = grad_b_parts(place, scales, after(shared, side_parts), sum(own, []))
    main_terms = over_rows(after(main_parts, side_terms))
    factor = small_call(
        factor_kernel, shape(piece[1:], BF16), (place, after(side_terms, keep_b))
    )
    got_b = swap(after(give_b, factor))
    hops = [factor] + [
        lax.ppermute(factor, "col", [(c, (c + 2 * hop) % 16) for c in range(16)])
        for hop in range(1, PLANES)
    ]
    hops[-1] = after(hops[-1], main_terms)
    factor_planes = small_call(
        stack_kernel, shape(piece, BF16), (place, *hops), scratch=(sems,)
    )

    part = (slots, height, feats)
    keep, give = small_call(
        main_kernel, (shape(part, F32), shape(part, F32)), (place, main_terms)
    )
    factor_tokens = over_rows(factor_planes)
    grad_in = small_call(
        grad_in_kernel,
        shape(x.shape, BF16),
        (place, factor_planes, swap(factor_planes), keep, swap(give), lefts),
    )
    grad_b = keep_b + got_b
    grad_a = small_call(
        grad_a_kernel,
        shape((slots, feats, 2 * ranks), F32),
        (place, scales, factor_tokens, swap(factor_tokens), shared),
    )
    return grad_in, grad_a, grad_b


def solution(mesh):
    return jax.shard_map(
        body,
        mesh=mesh,
        in_specs=(
            P("trial", "row", "col"),
            P("trial", "col", "row"),
            P("col", "row"),
            P("trial", "col", None),
            P("trial", "col", "row"),
            P("trial"),
            P("trial"),
        ),
        out_specs=(P("trial", "row", "col"), P("trial", "col", "row"), P("trial", "col", "row")),
        check_vma=False,
    )
```

```python
import jax
import jax.numpy as jnp
from jax import lax
from jax.experimental import pallas as pl
from jax.experimental.pallas import tpu as pltpu
from jax.sharding import PartitionSpec as P

ROWS = 8
PLANES = 8
SLOTS = 4
CHAINS = 2
F32 = jnp.float32
BF16 = jnp.bfloat16
RING = [(c, (c + 2) % 16) if c % 2 == 0 else (c, (c - 2) % 16) for c in range(16)]
SWAP = [(c, c ^ 1) for c in range(16)]
SAME_CORE = [list(range(0, 16, 2)), list(range(1, 16, 2))]
SMEM = pl.BlockSpec(memory_space=pltpu.SMEM)
VMEM = pl.BlockSpec(memory_space=pltpu.VMEM)
ANY = pl.BlockSpec(memory_space=pl.ANY)
MIB = 1024 * 1024
GUESS = pl.CostEstimate(flops=3 * 10**9, bytes_accessed=8 * MIB, transcendentals=0)


def dot_last(left, right):
    return lax.dot_general(
        left, right, (((1,), (1,)), ((), ())), preferred_element_type=F32
    )


def dot_first(left, right):
    return lax.dot_general(
        left, right, (((0,), (0,)), ((), ())), preferred_element_type=F32
    )


def origin_of(place, step):
    return lax.rem(place[0] + (2 * place[1] - 1) * step + PLANES, PLANES)


def keep_kernel(*refs):
    sems, refs = refs[-1], refs[:-1]
    count = len(refs) // 2
    copies = [
        pltpu.make_async_copy(refs[n], refs[count + n], sems.at[n]) for n in range(count)
    ]
    for copy in copies:
        copy.start()
    for copy in copies:
        copy.wait()


def kept_in_vmem(arrays):
    return pl.pallas_call(
        keep_kernel,
        out_shape=tuple(pltpu.VMEM(array.shape, array.dtype) for array in arrays),
        in_specs=[ANY] * len(arrays),
        out_specs=(VMEM,) * len(arrays),
        scratch_shapes=[pltpu.SemaphoreType.DMA((len(arrays),))],
        compiler_params=pltpu.CompilerParams(vmem_limit_bytes=24 * MIB),
        cost_estimate=GUESS,
    )(*arrays)


def step_kernel(steps, place, *refs):
    count = CHAINS * len(steps)
    units, weights = refs[:count], refs[count : count + 4]
    main_out, side_out, acc_c, acc_d, main, side, sems = refs[-7:]
    height = units[0].shape[1]
    rows = jnp.concatenate(
        [unit[n] for unit in units for n in range(SLOTS // CHAINS)], axis=0
    )
    acc_a = dot_last(rows, weights[0][...])
    acc_b = dot_last(rows, weights[1][...])
    for at in range(len(steps)):
        for slot in range(SLOTS):
            top = height * (SLOTS * at + slot)
            here = slice(top, top + height)
            both = jnp.concatenate([acc_a[here], acc_b[here]], axis=1)
            main[at, slot] = both.astype(BF16)
    copies = [
        pltpu.make_async_copy(
            main.at[at], main_out.at[origin_of(place, step)], sems.at[2 * at]
        )
        for at, step in enumerate(steps)
    ]
    for copy in copies:
        copy.start()
    acc_c[...] = dot_last(rows, weights[2][...])
    acc_d[...] = dot_last(rows, weights[3][...])
    half = acc_c.shape[1] // SLOTS
    for at, step in enumerate(steps):
        for slot in range(SLOTS):
            top = height * (SLOTS * at + slot)
            here = slice(top, top + height)
            entry = place[2 + slot]
            lanes = pl.ds(pl.multiple_of(entry // 2 * 2 * half, 2 * half), 2 * half)
            parts = []
            for acc in (acc_c, acc_d):
                pair = acc[here, lanes]
                parts.append(jnp.where(entry % 2 == 0, pair[:, :half], pair[:, half:]))
            side[at, slot] = jnp.concatenate(parts, axis=1).astype(BF16)
        copy = pltpu.make_async_copy(
            side.at[at], side_out.at[origin_of(place, step)], sems.at[1 + 2 * at]
        )
        copy.start()
        copies.append(copy)
    for copy in copies:
        copy.wait()


def step_products(steps, place, units, weights, done):
    height = units[0].shape[1]
    feats, ranks = weights[0].shape[0], weights[2].shape[0]
    count = len(units)
    rows = SLOTS * len(steps) * height
    main_shape = (SLOTS, height, 2 * feats)
    side_shape = (SLOTS, height, 2 * ranks // SLOTS)

    def kernel(*refs):
        step_kernel(steps, *refs)

    return pl.pallas_call(
        kernel,
        out_shape=(
            jax.ShapeDtypeStruct((ROWS,) + main_shape, BF16),
            jax.ShapeDtypeStruct((ROWS,) + side_shape, BF16),
        ),
        in_specs=[SMEM] + [VMEM] * (count + 4) + [ANY] * len(done),
        out_specs=(ANY, ANY),
        scratch_shapes=[
            pltpu.VMEM((rows, ranks), F32),
            pltpu.VMEM((rows, ranks), F32),
            pltpu.VMEM((len(steps),) + main_shape, BF16),
            pltpu.VMEM((len(steps),) + side_shape, BF16),
            pltpu.SemaphoreType.DMA((2 * len(steps),)),
        ],
        input_output_aliases={count + 5: 0, count + 6: 1} if done else {},
        compiler_params=pltpu.CompilerParams(vmem_limit_bytes=24 * MIB),
        cost_estimate=GUESS,
    )(place, *units, *weights, *done)


def small_call(kernel, out_shape, args, scratch=(), limit=24):
    scalars = sum(arg.ndim == 1 for arg in args)
    return pl.pallas_call(
        kernel,
        out_shape=out_shape,
        in_specs=[SMEM] * scalars + [VMEM] * (len(args) - scalars),
        out_specs=jax.tree.map(lambda _: VMEM if not scratch else ANY, out_shape),
        scratch_shapes=list(scratch),
        compiler_params=pltpu.CompilerParams(vmem_limit_bytes=limit * MIB),
        cost_estimate=GUESS,
    )(*args)


def pick(place, low, high):
    first = place[1] == 0
    return jnp.where(first, low, high), jnp.where(first, high, low)


def own_rows(place, height):
    start = pl.multiple_of(place[1] * height, height)
    return pl.ds(start, height)


def other_rows(place, height):
    start = pl.multiple_of((1 - place[1]) * height, height)
    return pl.ds(start, height)


def masked_sum(place, terms, slot):
    total = terms[0, slot].astype(F32)
    for source in range(1, ROWS):
        total = total + terms[source, slot].astype(F32)
    height = total.shape[0]
    start = 2 * height * place[6] + height * place[1]
    position = start + lax.broadcasted_iota(jnp.int32, total.shape, 0)
    return jnp.where(position < place[7 + slot], total, 0.0)


def send_to_all(stage, out, sems):
    copies = [pltpu.make_async_copy(stage, out.at[n], sems.at[n]) for n in range(8)]
    for copy in copies:
        copy.start()
    for copy in copies:
        copy.wait()


def hidden_kernel(place, x, lefts, keep, give):
    height, width = keep.shape[2:]
    for slot in range(SLOTS):
        both = jnp.dot(x[slot], lefts[place[2 + slot]], preferred_element_type=F32)
        mine, others = pick(place, both[:height], both[height:])
        for plane in range(PLANES):
            lanes = slice(width * plane, width * (plane + 1))
            keep[plane, slot] = mine[:, lanes]
            give[plane, slot] = others[:, lanes]


def share_kernel(place, terms, x, out, stage, sems):
    for slot in range(SLOTS):
        hidden = masked_sum(place, terms, slot).astype(BF16)
        half = hidden.shape[1] // 2
        stacked = jnp.concatenate([hidden[:, :half], hidden[:, half:]], axis=0)
        stage[slot] = jnp.concatenate([x[slot], stacked], axis=1)
    send_to_all(stage, out, sems)


def factor_kernel(place, terms, out):
    for slot in range(SLOTS):
        total = masked_sum(place, terms, slot)
        half = total.shape[1] // 2
        turned = jnp.concatenate([total[:, half:], total[:, :half]], axis=1)
        out[slot] = jnp.where(place[1] == 0, total, turned).astype(BF16)


def stack_kernel(place, *refs):
    pieces, (out, sems) = refs[:PLANES], refs[PLANES:]
    copies = []
    for hop, piece in enumerate(pieces):
        origin = lax.rem(place[0] - hop + PLANES, PLANES)
        copies.append(pltpu.make_async_copy(piece, out.at[origin], sems.at[hop]))
    for copy in copies:
        copy.start()
    for copy in copies:
        copy.wait()


def main_kernel(place, terms, keep, give):
    feats = keep.shape[-1]
    for slot in range(SLOTS):
        total = masked_sum(place, terms, slot)
        keep[slot] = total[:, :feats]
        give[slot] = total[:, feats:]


def grad_in_kernel(place, mine, others, keep, got, lefts, out):
    height = keep.shape[1]
    for slot in range(SLOTS):
        rows = jnp.concatenate(
            [
                jnp.concatenate([part[plane, slot] for plane in range(PLANES)], axis=1)
                for part in (mine, others)
            ],
            axis=0,
        )
        side = dot_last(rows, lefts[place[2 + slot]])
        out[slot, own_rows(place, height)] = (keep[slot] + side[:height]).astype(BF16)
        out[slot, other_rows(place, height)] = (got[slot] + side[height:]).astype(BF16)


def grad_a_kernel(place, scales, mine, others, shared, out):
    height = mine.shape[2]
    feats = out.shape[1]
    for slot in range(SLOTS):
        acts, factors = [], []
        for part, here in (
            (mine, own_rows(place, height)),
            (others, other_rows(place, height)),
        ):
            for row in range(ROWS):
                acts.append(shared[row, slot, here, :feats])
                factors.append(part[row, slot])
        acts = jnp.concatenate(acts, axis=0)
        factors = jnp.concatenate(factors, axis=0)
        out[place[2 + slot]] = dot_first(acts, factors) * scales[slot]


def grad_b_kernel(place, scales, shared, *refs):
    units, (keep, give, rows, sems) = refs[:-4], refs[-4:]
    ranks = keep.shape[1]
    height = units[0].shape[1]
    feats = shared.shape[-1] - ranks
    loads = []
    for slot in range(SLOTS):
        for step in range(PLANES):
            here = pl.ds(height * step, height)
            pair = SLOTS // CHAINS
            unit = units[CHAINS * step + slot // pair].at[slot % pair]
            sem = sems.at[PLANES * slot + step]
            loads.append(pltpu.make_async_copy(unit, rows.at[slot, here], sem))
    for load in loads:
        load.start()
    for slot in range(SLOTS):
        hidden = []
        for step in range(PLANES):
            origin = origin_of(place, step)
            pair = [
                shared[origin, slot, here, feats:]
                for here in (own_rows(place, height), other_rows(place, height))
            ]
            hidden.append(jnp.concatenate(pair, axis=1))
            loads[PLANES * slot + step].wait()
        both = dot_first(jnp.concatenate(hidden, axis=0), rows[slot]) * scales[slot]
        entry = place[2 + slot]
        keep[entry] = both[:ranks]
        give[entry] = both[ranks:]


def grad_b_parts(place, scales, shared, units):
    height, depth = units[0].shape[1:]
    ranks = shared.shape[2]
    part = jax.ShapeDtypeStruct((SLOTS, ranks, depth), F32)
    return pl.pallas_call(
        grad_b_kernel,
        out_shape=(part, part),
        in_specs=[SMEM, SMEM, VMEM] + [ANY] * len(units),
        out_specs=(VMEM, VMEM),
        scratch_shapes=[
            pltpu.VMEM((SLOTS, PLANES * height, depth), BF16),
            pltpu.SemaphoreType.DMA((SLOTS * PLANES,)),
        ],
        compiler_params=pltpu.CompilerParams(vmem_limit_bytes=60 * MIB),
        cost_estimate=GUESS,
    )(place, scales, shared, *units)


def body(x, dy, weight, lefts, rights, chosen, counts):
    slots, tokens, feats = x.shape
    height, depth = dy.shape[1:]
    ranks = rights.shape[1]
    col = lax.axis_index("col")
    row = lax.axis_index("row")
    plane, core = col // 2, col % 2

    def swap(piece):
        return lax.ppermute(piece, "col", SWAP)

    def over_planes(pieces):
        return lax.all_to_all(pieces, "col", 0, 0, axis_index_groups=SAME_CORE)

    def over_rows(pieces):
        return lax.all_to_all(pieces, "row", 0, 0)

    def after(value, *earlier):
        return lax.optimization_barrier((value,) + earlier)[0]

    def passed_on(units):
        return [lax.ppermute(unit, "col", RING) for unit in units]

    shape = jax.ShapeDtypeStruct
    sems = pltpu.SemaphoreType.DMA((8,))
    entry = chosen - lax.axis_index("trial") * slots
    scales = lax.rsqrt(counts.astype(F32))
    place = jnp.concatenate([jnp.stack([plane, core]), entry, row[None], counts])
    place = place.astype(jnp.int32)

    pair = slots // CHAINS
    own = [[dy[pair * n : pair * (n + 1)] for n in range(CHAINS)]]
    own.append(passed_on(own[0]))
    ups = after(rights.reshape(slots * ranks, depth), *own[1])
    weight = after(weight, *own[1])
    weights = [weight, swap(weight), ups, swap(ups)]
    own.append(passed_on(own[1]))

    piece = (PLANES, slots, height, 2 * ranks)
    keep, give = small_call(
        hidden_kernel,
        (shape(piece, F32), shape(piece, F32)),
        (place, after(x, *own[0]), lefts),
    )
    mixed = (keep + swap(give)).astype(BF16)
    terms = over_planes(mixed)
    own.append(passed_on(own[2]))
    own[3][1] = after(own[3][1], terms)
    own.append(passed_on(own[3]))
    wide = (slots, tokens, feats + ranks)
    shared = small_call(
        share_kernel,
        shape((ROWS,) + wide, BF16),
        (place, terms, x),
        scratch=(pltpu.VMEM(wide, BF16), sems),
    )
    own[4][1] = after(own[4][1], shared)
    shared = over_rows(shared)
    own.append(passed_on(own[4]))
    weights = kept_in_vmem(weights)
    products = step_products((0, 1, 2, 3), place, sum(own[:4], []), weights, ())
    own[5][0] = after(own[5][0], *products)
    own.append(passed_on(own[5]))
    products = step_products((4, 5), place, own[4] + own[5], weights, products)
    own[6][1] = after(own[6][1], *products)
    own.append(passed_on(own[6]))
    products = step_products((6, 7), place, own[6] + own[7], weights, products)
    main_parts, side_parts = products

    side_terms = over_rows(after(side_parts, shared))
    keep_b, give_b = grad_b_parts(place, scales, after(shared, side_parts), sum(own, []))
    main_terms = over_rows(after(main_parts, side_terms))
    factor = small_call(
        factor_kernel, shape(piece[1:], BF16), (place, after(side_terms, keep_b))
    )
    got_b = swap(after(give_b, factor))
    hops = [factor] + [
        lax.ppermute(factor, "col", [(c, (c + 2 * hop) % 16) for c in range(16)])
        for hop in range(1, PLANES)
    ]
    hops[-1] = after(hops[-1], main_terms)
    factor_planes = small_call(
        stack_kernel, shape(piece, BF16), (place, *hops), scratch=(sems,)
    )

    part = (slots, height, feats)
    keep, give = small_call(
        main_kernel, (shape(part, F32), shape(part, F32)), (place, main_terms)
    )
    factor_tokens = over_rows(factor_planes)
    grad_in = small_call(
        grad_in_kernel,
        shape(x.shape, BF16),
        (place, factor_planes, swap(factor_planes), keep, swap(give), lefts),
    )
    grad_b = keep_b + got_b
    factor_tokens = after(factor_tokens, grad_in, grad_b)
    grad_a = small_call(
        grad_a_kernel,
        shape((slots, feats, 2 * ranks), F32),
        (place, scales, factor_tokens, swap(factor_tokens), shared),
    )
    return grad_in, grad_a, grad_b


def solution(mesh):
    return jax.shard_map(
        body,
        mesh=mesh,
        in_specs=(
            P("trial", "row", "col"),
            P("trial", "col", "row"),
            P("col", "row"),
            P("trial", "col", None),
            P("trial", "col", "row"),
            P("trial"),
            P("trial"),
        ),
        out_specs=(P("trial", "row", "col"), P("trial", "col", "row"), P("trial", "col", "row")),
        check_vma=False,
    )
```

```python
import jax
import jax.numpy as jnp
from jax import lax
from jax.experimental import pallas as pl
from jax.experimental.pallas import tpu as pltpu
from jax.sharding import PartitionSpec as P

ROWS = 8
PLANES = 8
SLOTS = 4
CHAINS = 2
F32 = jnp.float32
BF16 = jnp.bfloat16
RING = [(c, (c + 2) % 16) if c % 2 == 0 else (c, (c - 2) % 16) for c in range(16)]
SWAP = [(c, c ^ 1) for c in range(16)]
SAME_CORE = [list(range(0, 16, 2)), list(range(1, 16, 2))]
SMEM = pl.BlockSpec(memory_space=pltpu.SMEM)
VMEM = pl.BlockSpec(memory_space=pltpu.VMEM)
ANY = pl.BlockSpec(memory_space=pl.ANY)
MIB = 1024 * 1024
GUESS = pl.CostEstimate(flops=3 * 10**9, bytes_accessed=8 * MIB, transcendentals=0)


def dot_last(left, right):
    return lax.dot_general(
        left, right, (((1,), (1,)), ((), ())), preferred_element_type=F32
    )


def dot_first(left, right):
    return lax.dot_general(
        left, right, (((0,), (0,)), ((), ())), preferred_element_type=F32
    )


def origin_of(place, step):
    return lax.rem(place[0] + (2 * place[1] - 1) * step + PLANES, PLANES)


def keep_kernel(*refs):
    sems, refs = refs[-1], refs[:-1]
    count = len(refs) // 2
    copies = [
        pltpu.make_async_copy(refs[n], refs[count + n], sems.at[n]) for n in range(count)
    ]
    for copy in copies:
        copy.start()
    for copy in copies:
        copy.wait()


def kept_in_vmem(arrays):
    return pl.pallas_call(
        keep_kernel,
        out_shape=tuple(pltpu.VMEM(array.shape, array.dtype) for array in arrays),
        in_specs=[ANY] * len(arrays),
        out_specs=(VMEM,) * len(arrays),
        scratch_shapes=[pltpu.SemaphoreType.DMA((len(arrays),))],
        compiler_params=pltpu.CompilerParams(vmem_limit_bytes=24 * MIB),
        cost_estimate=GUESS,
    )(*arrays)


def step_kernel(steps, place, *refs):
    count = CHAINS * len(steps)
    units, weights = refs[:count], refs[count : count + 4]
    main_out, side_out, acc_c, acc_d, main, side, sems = refs[-7:]
    height = units[0].shape[1]
    rows = jnp.concatenate(
        [unit[n] for unit in units for n in range(SLOTS // CHAINS)], axis=0
    )
    acc_a = dot_last(rows, weights[0][...])
    acc_b = dot_last(rows, weights[1][...])
    for at in range(len(steps)):
        for slot in range(SLOTS):
            top = height * (SLOTS * at + slot)
            here = slice(top, top + height)
            both = jnp.concatenate([acc_a[here], acc_b[here]], axis=1)
            main[at, slot] = both.astype(BF16)
    copies = [
        pltpu.make_async_copy(
            main.at[at], main_out.at[origin_of(place, step)], sems.at[2 * at]
        )
        for at, step in enumerate(steps)
    ]
    for copy in copies:
        copy.start()
    acc_c[...] = dot_last(rows, weights[2][...])
    acc_d[...] = dot_last(rows, weights[3][...])
    half = acc_c.shape[1] // SLOTS
    for at, step in enumerate(steps):
        for slot in range(SLOTS):
            top = height * (SLOTS * at + slot)
            here = slice(top, top + height)
            entry = place[2 + slot]
            lanes = pl.ds(pl.multiple_of(entry // 2 * 2 * half, 2 * half), 2 * half)
            parts = []
            for acc in (acc_c, acc_d):
                pair = acc[here, lanes]
                parts.append(jnp.where(entry % 2 == 0, pair[:, :half], pair[:, half:]))
            side[at, slot] = jnp.concatenate(parts, axis=1).astype(BF16)
        copy = pltpu.make_async_copy(
            side.at[at], side_out.at[origin_of(place, step)], sems.at[1 + 2 * at]
        )
        copy.start()
        copies.append(copy)
    for copy in copies:
        copy.wait()


def step_products(steps, place, units, weights, done):
    height = units[0].shape[1]
    feats, ranks = weights[0].shape[0], weights[2].shape[0]
    count = len(units)
    rows = SLOTS * len(steps) * height
    main_shape = (SLOTS, height, 2 * feats)
    side_shape = (SLOTS, height, 2 * ranks // SLOTS)

    def kernel(*refs):
        step_kernel(steps, *refs)

    return pl.pallas_call(
        kernel,
        out_shape=(
            jax.ShapeDtypeStruct((ROWS,) + main_shape, BF16),
            jax.ShapeDtypeStruct((ROWS,) + side_shape, BF16),
        ),
        in_specs=[SMEM] + [VMEM] * (count + 4) + [ANY] * len(done),
        out_specs=(ANY, ANY),
        scratch_shapes=[
            pltpu.VMEM((rows, ranks), F32),
            pltpu.VMEM((rows, ranks), F32),
            pltpu.VMEM((len(steps),) + main_shape, BF16),
            pltpu.VMEM((len(steps),) + side_shape, BF16),
            pltpu.SemaphoreType.DMA((2 * len(steps),)),
        ],
        input_output_aliases={count + 5: 0, count + 6: 1} if done else {},
        compiler_params=pltpu.CompilerParams(vmem_limit_bytes=24 * MIB),
        cost_estimate=GUESS,
    )(place, *units, *weights, *done)


def small_call(kernel, out_shape, args, scratch=(), limit=24):
    scalars = sum(arg.ndim == 1 for arg in args)
    return pl.pallas_call(
        kernel,
        out_shape=out_shape,
        in_specs=[SMEM] * scalars + [VMEM] * (len(args) - scalars),
        out_specs=jax.tree.map(lambda _: VMEM if not scratch else ANY, out_shape),
        scratch_shapes=list(scratch),
        compiler_params=pltpu.CompilerParams(vmem_limit_bytes=limit * MIB),
        cost_estimate=GUESS,
    )(*args)


def pick(place, low, high):
    first = place[1] == 0
    return jnp.where(first, low, high), jnp.where(first, high, low)


def own_rows(place, height):
    start = pl.multiple_of(place[1] * height, height)
    return pl.ds(start, height)


def other_rows(place, height):
    start = pl.multiple_of((1 - place[1]) * height, height)
    return pl.ds(start, height)


def masked_sum(place, terms, slot):
    total = terms[0, slot].astype(F32)
    for source in range(1, ROWS):
        total = total + terms[source, slot].astype(F32)
    height = total.shape[0]
    start = 2 * height * place[6] + height * place[1]
    position = start + lax.broadcasted_iota(jnp.int32, total.shape, 0)
    return jnp.where(position < place[7 + slot], total, 0.0)


def send_to_all(stage, out, sems):
    copies = [pltpu.make_async_copy(stage, out.at[n], sems.at[n]) for n in range(8)]
    for copy in copies:
        copy.start()
    for copy in copies:
        copy.wait()


def hidden_kernel(place, x, lefts, keep, give):
    height, width = keep.shape[2:]
    for slot in range(SLOTS):
        both = jnp.dot(x[slot], lefts[place[2 + slot]], preferred_element_type=F32)
        mine, others = pick(place, both[:height], both[height:])
        for plane in range(PLANES):
            lanes = slice(width * plane, width * (plane + 1))
            keep[plane, slot] = mine[:, lanes]
            give[plane, slot] = others[:, lanes]


def share_kernel(place, terms, x, out, stage, sems):
    for slot in range(SLOTS):
        hidden = masked_sum(place, terms, slot).astype(BF16)
        half = hidden.shape[1] // 2
        stacked = jnp.concatenate([hidden[:, :half], hidden[:, half:]], axis=0)
        stage[slot] = jnp.concatenate([x[slot], stacked], axis=1)
    send_to_all(stage, out, sems)


def factor_kernel(place, terms, out):
    for slot in range(SLOTS):
        total = masked_sum(place, terms, slot)
        half = total.shape[1] // 2
        turned = jnp.concatenate([total[:, half:], total[:, :half]], axis=1)
        out[slot] = jnp.where(place[1] == 0, total, turned).astype(BF16)


def stack_kernel(place, *refs):
    pieces, (out, sems) = refs[:PLANES], refs[PLANES:]
    copies = []
    for hop, piece in enumerate(pieces):
        origin = lax.rem(place[0] - hop + PLANES, PLANES)
        copies.append(pltpu.make_async_copy(piece, out.at[origin], sems.at[hop]))
    for copy in copies:
        copy.start()
    for copy in copies:
        copy.wait()


def main_kernel(place, terms, keep, give):
    feats = keep.shape[-1]
    for slot in range(SLOTS):
        total = masked_sum(place, terms, slot)
        keep[slot] = total[:, :feats]
        give[slot] = total[:, feats:]


def grad_in_kernel(place, mine, others, keep, got, lefts, out):
    height = keep.shape[1]
    for slot in range(SLOTS):
        rows = jnp.concatenate(
            [
                jnp.concatenate([part[plane, slot] for plane in range(PLANES)], axis=1)
                for part in (mine, others)
            ],
            axis=0,
        )
        side = dot_last(rows, lefts[place[2 + slot]])
        out[slot, own_rows(place, height)] = (keep[slot] + side[:height]).astype(BF16)
        out[slot, other_rows(place, height)] = (got[slot] + side[height:]).astype(BF16)


def grad_a_kernel(place, scales, mine, others, shared, out):
    height = mine.shape[2]
    feats = out.shape[1]
    for slot in range(SLOTS):
        acts, factors = [], []
        for part, here in (
            (mine, own_rows(place, height)),
            (others, other_rows(place, height)),
        ):
            for row in range(ROWS):
                acts.append(shared[row, slot, here, :feats])
                factors.append(part[row, slot])
        acts = jnp.concatenate(acts, axis=0)
        factors = jnp.concatenate(factors, axis=0)
        out[place[2 + slot]] = dot_first(acts, factors) * scales[slot]


def grad_b_kernel(place, scales, shared, *refs):
    units, (keep, give, rows, sems) = refs[:-4], refs[-4:]
    ranks = keep.shape[1]
    height = units[0].shape[1]
    feats = shared.shape[-1] - ranks
    loads = []
    for slot in range(SLOTS):
        for step in range(PLANES):
            here = pl.ds(height * step, height)
            pair = SLOTS // CHAINS
            unit = units[CHAINS * step + slot // pair].at[slot % pair]
            sem = sems.at[PLANES * slot + step]
            loads.append(pltpu.make_async_copy(unit, rows.at[slot, here], sem))
    for load in loads:
        load.start()
    for slot in range(SLOTS):
        hidden = []
        for step in range(PLANES):
            origin = origin_of(place, step)
            pair = [
                shared[origin, slot, here, feats:]
                for here in (own_rows(place, height), other_rows(place, height))
            ]
            hidden.append(jnp.concatenate(pair, axis=1))
            loads[PLANES * slot + step].wait()
        both = dot_first(jnp.concatenate(hidden, axis=0), rows[slot]) * scales[slot]
        entry = place[2 + slot]
        keep[entry] = both[:ranks]
        give[entry] = both[ranks:]


def grad_b_parts(place, scales, shared, units):
    height, depth = units[0].shape[1:]
    ranks = shared.shape[2]
    part = jax.ShapeDtypeStruct((SLOTS, ranks, depth), F32)
    return pl.pallas_call(
        grad_b_kernel,
        out_shape=(part, part),
        in_specs=[SMEM, SMEM, VMEM] + [ANY] * len(units),
        out_specs=(VMEM, VMEM),
        scratch_shapes=[
            pltpu.VMEM((SLOTS, PLANES * height, depth), BF16),
            pltpu.SemaphoreType.DMA((SLOTS * PLANES,)),
        ],
        compiler_params=pltpu.CompilerParams(vmem_limit_bytes=60 * MIB),
        cost_estimate=GUESS,
    )(place, scales, shared, *units)


def body(x, dy, weight, lefts, rights, chosen, counts):
    slots, tokens, feats = x.shape
    height, depth = dy.shape[1:]
    ranks = rights.shape[1]
    col = lax.axis_index("col")
    row = lax.axis_index("row")
    plane, core = col // 2, col % 2

    def swap(piece):
        return lax.ppermute(piece, "col", SWAP)

    def over_planes(pieces):
        return lax.all_to_all(pieces, "col", 0, 0, axis_index_groups=SAME_CORE)

    def over_rows(pieces):
        return lax.all_to_all(pieces, "row", 0, 0)

    def after(value, *earlier):
        return lax.optimization_barrier((value,) + earlier)[0]

    def passed_on(units):
        return [lax.ppermute(unit, "col", RING) for unit in units]

    shape = jax.ShapeDtypeStruct
    sems = pltpu.SemaphoreType.DMA((8,))
    entry = chosen - lax.axis_index("trial") * slots
    scales = lax.rsqrt(counts.astype(F32))
    place = jnp.concatenate([jnp.stack([plane, core]), entry, row[None], counts])
    place = place.astype(jnp.int32)

    pair = slots // CHAINS
    own = [[dy[pair * n : pair * (n + 1)] for n in range(CHAINS)]]
    own.append(passed_on(own[0]))
    ups = after(rights.reshape(slots * ranks, depth), *own[1])
    weight = after(weight, *own[1])
    weights = [weight, swap(weight), ups, swap(ups)]
    own.append(passed_on(own[1]))

    piece = (PLANES, slots, height, 2 * ranks)
    keep, give = small_call(
        hidden_kernel,
        (shape(piece, F32), shape(piece, F32)),
        (place, after(x, *own[0]), lefts),
    )
    mixed = (keep + swap(give)).astype(BF16)
    terms = over_planes(mixed)
    own.append(passed_on(own[2]))
    own[3][1] = after(own[3][1], terms)
    own.append(passed_on(own[3]))
    wide = (slots, tokens, feats + ranks)
    shared = small_call(
        share_kernel,
        shape((ROWS,) + wide, BF16),
        (place, terms, x),
        scratch=(pltpu.VMEM(wide, BF16), sems),
    )
    own[4][1] = after(own[4][1], shared)
    shared = over_rows(shared)
    own.append(passed_on(own[4]))
    weights = kept_in_vmem(weights)
    products = step_products((0, 1, 2, 3), place, sum(own[:4], []), weights, ())
    own[5][0] = after(own[5][0], *products)
    own.append(passed_on(own[5]))
    own.append(passed_on(own[6]))
    units = own[4] + own[5] + own[6]
    products = step_products((4, 5, 6), place, units, weights, products)
    products = step_products((7,), place, own[7], weights, products)
    main_parts, side_parts = products

    side_terms = over_rows(after(side_parts, shared))
    keep_b, give_b = grad_b_parts(place, scales, after(shared, side_parts), sum(own, []))
    main_terms = over_rows(after(main_parts, side_terms))
    factor = small_call(
        factor_kernel, shape(piece[1:], BF16), (place, after(side_terms, keep_b))
    )
    got_b = swap(after(give_b, factor))
    hops = [factor] + [
        lax.ppermute(factor, "col", [(c, (c + 2 * hop) % 16) for c in range(16)])
        for hop in range(1, PLANES)
    ]
    hops[-1] = after(hops[-1], main_terms)
    factor_planes = small_call(
        stack_kernel, shape(piece, BF16), (place, *hops), scratch=(sems,)
    )

    part = (slots, height, feats)
    keep, give = small_call(
        main_kernel, (shape(part, F32), shape(part, F32)), (place, main_terms)
    )
    factor_tokens = over_rows(factor_planes)
    grad_in = small_call(
        grad_in_kernel,
        shape(x.shape, BF16),
        (place, factor_planes, swap(factor_planes), keep, swap(give), lefts),
    )
    grad_b = keep_b + got_b
    factor_tokens = after(factor_tokens, grad_in, grad_b)
    grad_a = small_call(
        grad_a_kernel,
        shape((slots, feats, 2 * ranks), F32),
        (place, scales, factor_tokens, swap(factor_tokens), shared),
    )
    return grad_in, grad_a, grad_b


def solution(mesh):
    return jax.shard_map(
        body,
        mesh=mesh,
        in_specs=(
            P("trial", "row", "col"),
            P("trial", "col", "row"),
            P("col", "row"),
            P("trial", "col", None),
            P("trial", "col", "row"),
            P("trial"),
            P("trial"),
        ),
        out_specs=(P("trial", "row", "col"), P("trial", "col", "row"), P("trial", "col", "row")),
        check_vma=False,
    )
```
